128 devices in a mesh: gx: 4 (over z), gy: 32 (over y, x, core).
Axes of the slice: x: 4, y: 4, z: 4, core: 2. Of those that a mesh axis runs over, the one named last changes fastest.
Arguments:
- atm_fields: bfloat16 [4096, 512, 128], P(('gx', 'gy')), may hold values from -6 to 6
- neighbours: int32 [4096, 4], P(('gx', 'gy')), may hold values from 0 to 4095, as said below
- send_slots: int32 [128, 32, 2], P(('gx', 'gy')), may hold values from 0 to 31, as said below
- send_counts: int32 [128, 32], P(('gx', 'gy')), may hold values from 0 to 2, as said below
- tile_weights: bfloat16 [16384, 384, 128], P(('gx', 'gy')), may hold values from -0.109375 to 0.109375
- tile_rows: int32 [16384], P(('gx', 'gy')), may hold values from 0 to 7
- tile_cols: int32 [16384], P(('gx', 'gy')), may hold values from 0 to 63, as said below
Outputs:
- ocean_fields: bfloat16 [1024, 512, 128], P(('gx', 'gy'))
The draws below stay inside these ranges and needn't reach their ends.
Inputs may be any that keep to these rules, and one draw needn't show every extreme that they name: `neighbours`: each neighbour lies within 8 blocks of its block along the curve, and that distance is reached. `send_slots`: the live slots of a device name distinct blocks of it; every block of a device is in exactly one live slot. `send_counts`: A device's counts sum to 32; every device fills all 2 slots to some owner. `tile_cols`: each of the 64 received slots of a device is named by exactly two of its tiles.
All inputs are finite; a program needn't handle non-finite values.
Results may differ from the reference program's by a relative error of at most 0.0041.
Values may be sent and summed in bfloat16 or wider, within the bound.
No kernel may reach another device: no remote copies, remote signals or barrier semaphores. Data moves between devices by JAX's collectives and lax.ppermute only.
A program may use at most 192 MiB of HBM per device.

```python
import jax
import jax.numpy as jnp
from jax import lax

CELLS = 128
NA = 32
COLS = 512
CAP = 2
HALO = 8
NO = 8
NT = 128
NB = 4096
NOB = 1024
NTT = 16384
N_GX = 4
N_GY = 32
DEVICES = 128


def routing(key):
    key_hub, key_perm, key_offset, key_fill = jax.random.split(jax.random.fold_in(key, 11), 4)
    hubs = jax.random.randint(key_hub, (N_GX,), 0, N_GY)
    perms = jax.vmap(lambda single: jax.random.permutation(single, NA))(jax.random.split(key_perm, DEVICES))
    offsets = jax.random.randint(key_offset, (DEVICES,), 0, N_GY - 1)
    device = jnp.arange(DEVICES)
    hub = hubs[device // N_GY]
    position = jnp.arange(NA)
    shifted = jnp.broadcast_to(jnp.maximum(position[None, :] - CAP, 0), (DEVICES, NA))
    other_peer = (hub[:, None] + 1 + (offsets[:, None] + shifted) % (N_GY - 1)) % N_GY
    peer = jnp.where(position[None, :] < CAP, hub[:, None], other_peer)
    slot = jnp.where(position[None, :] < CAP, position[None, :], shifted // (N_GY - 1))
    table = jax.random.randint(key_fill, (DEVICES, N_GY, CAP), 0, NA)
    rows = jnp.broadcast_to(device[:, None], (DEVICES, NA))
    table = table.at[rows, peer, slot].set(perms)
    counts = jnp.zeros((DEVICES, N_GY), jnp.int32).at[rows, peer].add(1)
    return (table.astype(jnp.int32), counts)


def draw_send_slots(key, part):
    table, counts = routing(key)
    return table


def draw_send_counts(key, part):
    table, counts = routing(key)
    return counts


def draw_neighbours(key, part):
    key = jax.random.fold_in(key, 5)
    key_dist, key_sign = jax.random.split(key)
    blocks = jnp.arange(NB)
    distance = jax.random.randint(key_dist, (NB, 4), 1, HALO + 1)
    marked = blocks % NA == NA // 2
    distance = distance.at[:, 0].set(jnp.where(marked, HALO, distance[:, 0]))
    distance = distance.at[:, 1].set(jnp.where(marked, HALO, distance[:, 1]))
    flip = jax.random.randint(key_sign, (NB,), 0, 2) * 2 - 1
    signs = jnp.stack([jnp.ones_like(flip), -jnp.ones_like(flip), flip, -flip], axis=1)
    result = jnp.clip(blocks[:, None] + distance * signs, 0, NB - 1)
    return result.astype(jnp.int32)


def draw_tile_cols(key, part):
    key = jax.random.fold_in(key, 7)
    perms = jax.vmap(lambda single: jax.random.permutation(single, NT))(jax.random.split(key, DEVICES))
    return (perms // 2).reshape(-1).astype(jnp.int32)


def set_ends(values, own_key, low, high):
    extent = values.shape
    spot = [jax.random.randint(jax.random.fold_in(own_key, axis), (), 0, extent[axis]) for axis in range(len(extent))]
    values = values.at[tuple(spot)].set(low)
    longest = extent.index(max(extent))
    spot[longest] = (spot[longest] + 1) % extent[longest]
    return values.at[tuple(spot)].set(high)


def level_of(own_key, extent, shards, low, largest):
    def one(dim, shards_of):
        draws = jax.random.uniform(jax.random.fold_in(jax.random.fold_in(own_key, 6), dim), (shards_of,), jnp.float32, low / len(shards), largest / len(shards))
        return jnp.repeat(jnp.exp(draws), extent[dim] // shards_of).reshape((-1,) + (1,) * (len(extent) - dim - 1))

    gain = one(*shards[0])
    for cut in shards[1:]:
        gain = gain * one(*cut)
    return gain


def bell_draw(rng, dims, deviation, most, pieces=(), kind=jnp.bfloat16):
    level = level_of(rng, dims, pieces, -0.22, 0.18) if pieces else 1.0
    drawn = jax.random.normal(rng, dims, jnp.float32) * deviation * level
    return jnp.minimum(jnp.maximum(drawn, -most), most).astype(kind)


def setup_inputs(seed: int = 0) -> dict:
    keys = jax.random.split(jax.random.key(seed), 8)
    return {
        "atm_fields": bell_draw(keys[0], (NB, COLS, CELLS), 1.0, 6.0, ((0, 128),)),
        "neighbours": draw_neighbours(jax.random.fold_in(keys[7], 71), 0),
        "send_slots": draw_send_slots(jax.random.fold_in(keys[7], 71), 0),
        "send_counts": draw_send_counts(jax.random.fold_in(keys[7], 71), 0),
        "tile_weights": bell_draw(keys[4], (NTT, 3 * CELLS, CELLS), (24 * CELLS) ** -0.5, 0.109375, ((0, 128),)),
        "tile_rows": set_ends(jax.random.randint(keys[5], (NTT,), 0, NO), jax.random.fold_in(keys[5], 1), 0, NO - 1).astype(jnp.int32),
        "tile_cols": draw_tile_cols(jax.random.fold_in(keys[7], 71), 0),
    }


def reference(atm_fields, neighbours, send_slots, send_counts, tile_weights, tile_rows, tile_cols):
    def one_device(device):
        group_first = (device // N_GY) * N_GY
        position = device % N_GY
        sources = (group_first + jnp.arange(N_GY)).astype(jnp.int32)
        slot_table = send_slots[sources, position]
        planned = send_counts[sources, position]
        global_block = (sources[:, None] * NA + slot_table).reshape(-1).astype(jnp.int32)
        values = atm_fields[global_block]
        near = neighbours[global_block]
        east_side = atm_fields[near[:, 0]].astype(jnp.float32)
        west_side = atm_fields[near[:, 1]].astype(jnp.float32)
        north_side = atm_fields[near[:, 2]].astype(jnp.float32)
        south_side = atm_fields[near[:, 3]].astype(jnp.float32)
        grad_x = (0.5 * (east_side - west_side)).astype(jnp.bfloat16)
        grad_y = (0.5 * (north_side - south_side)).astype(jnp.bfloat16)
        payload = jnp.concatenate([values, grad_x, grad_y], axis=2)
        occupied = (jnp.arange(CAP)[None, :] < planned[:, None]).reshape(-1)
        payload = jnp.where(occupied[:, None, None], payload, jnp.zeros_like(payload))
        start = (device * NT).astype(jnp.int32)
        weights = lax.dynamic_slice_in_dim(tile_weights, start, NT, 0).astype(jnp.float32)
        row_index = lax.dynamic_slice_in_dim(tile_rows, start, NT, 0)
        column_index = lax.dynamic_slice_in_dim(tile_cols, start, NT, 0)
        chosen = payload[column_index].astype(jnp.float32)
        products = jnp.einsum("tcj,tjk->tck", chosen, weights, precision=lax.Precision.HIGHEST)
        total = jax.ops.segment_sum(products, row_index, num_segments=NO)
        return total.astype(jnp.bfloat16)

    result = lax.map(one_device, jnp.arange(DEVICES).astype(jnp.int32))
    return result.reshape(NOB, COLS, CELLS)
```

```python
import functools

import jax
import jax.numpy as jnp
from jax import lax
from jax.experimental import pallas as pl
from jax.experimental.pallas import tpu as pltpu
from jax.sharding import PartitionSpec as P

VMEM_LIMIT = 48 * 1024 * 1024
DEPTH = 8
NOTE = 16


def any_spec():
    return pl.BlockSpec(memory_space=pl.ANY)


def smem_spec():
    return pl.BlockSpec(memory_space=pltpu.SMEM)


def neighbour_blocks(block, width):
    axes = ("gx", "gy")
    count = lax.axis_size(axes)
    forward = [(i, i + 1) for i in range(count - 1)]
    backward = [(target, source) for source, target in forward]
    low = lax.ppermute(block[-width:], axes, forward)
    high = lax.ppermute(block[:width], axes, backward)
    return low, high


def order_kernel(slots, note, source, target, held, sems):
    count = target.shape[0]
    columns = source.shape[1]
    held[:, columns:, :] = jnp.broadcast_to(note[...][:, None, :], (count, NOTE, note.shape[1]))

    def fetch(i):
        return pltpu.make_async_copy(
            source.at[slots[i]], held.at[i, pl.ds(0, columns)], sems.at[0, i]
        )

    def store(i):
        return pltpu.make_async_copy(held.at[i], target.at[i], sems.at[1, i])

    def begin(i, carry):
        fetch(i).start()
        return carry

    def turn(i, carry):
        fetch(i).wait()
        store(i).start()
        return carry

    def end(i, carry):
        store(i).wait()
        return carry

    lax.fori_loop(0, count, begin, 0)
    lax.fori_loop(0, count, turn, 0)
    lax.fori_loop(0, count, end, 0)


def in_order(blocks, slots, note):
    count = slots.shape[0]
    shape = (count, blocks.shape[1] + NOTE, blocks.shape[2])
    return pl.pallas_call(
        order_kernel,
        out_shape=jax.ShapeDtypeStruct(shape, blocks.dtype),
        in_specs=[smem_spec(), pl.BlockSpec(memory_space=pltpu.VMEM), any_spec()],
        out_specs=any_spec(),
        scratch_shapes=[
            pltpu.VMEM(shape, blocks.dtype),
            pltpu.SemaphoreType.DMA((2, count)),
        ],
        compiler_params=pltpu.CompilerParams(vmem_limit_bytes=VMEM_LIMIT),
        cost_estimate=pl.CostEstimate(
            flops=0, transcendentals=0, bytes_accessed=4 * count * shape[1] * shape[2]
        ),
        name="order",
    )(slots, note, blocks)


def gradient_kernel(slots, near, low, own, high, target, held, made, sems, out_sems):
    count, columns, cells = own.shape
    width = low.shape[0]
    steps = target.shape[0]
    copies = [
        pltpu.make_async_copy(low, held.at[pl.ds(0, width)], sems.at[0]),
        pltpu.make_async_copy(own, held.at[pl.ds(width, count)], sems.at[1]),
        pltpu.make_async_copy(high, held.at[pl.ds(width + count, width)], sems.at[2]),
    ]
    for copy in copies:
        copy.start()
    for copy in copies:
        copy.wait()

    def make(i):
        block = slots[i]
        for axis in range(2):
            first = near[4 * block + 2 * axis]
            second = near[4 * block + 2 * axis + 1]
            for begin in range(0, columns, 128):
                rows = pl.ds(begin, 128)
                a = held[first, rows, :].astype(jnp.float32)
                b = held[second, rows, :].astype(jnp.float32)
                made[i, rows, axis * cells : (axis + 1) * cells] = (0.5 * (a - b)).astype(made.dtype)

    def store(i):
        return pltpu.make_async_copy(made.at[i], target.at[i], out_sems.at[i])

    def turn(i, carry):
        make(i)
        store(i).start()
        return carry

    def end(i, carry):
        store(i).wait()
        return carry

    lax.fori_loop(0, steps, turn, 0)
    lax.fori_loop(0, steps, end, 0)


def gradients(slots, near, low, own, high):
    width = low.shape[0]
    count, columns, cells = own.shape
    steps = slots.shape[0]
    return pl.pallas_call(
        gradient_kernel,
        out_shape=jax.ShapeDtypeStruct((steps, columns, 2 * cells), own.dtype),
        in_specs=[smem_spec(), smem_spec()] + [any_spec()] * 3,
        out_specs=any_spec(),
        scratch_shapes=[
            pltpu.VMEM((count + 2 * width, columns, cells), own.dtype),
            pltpu.VMEM((steps, columns, 2 * cells), own.dtype),
            pltpu.SemaphoreType.DMA((3,)),
            pltpu.SemaphoreType.DMA((steps,)),
        ],
        compiler_params=pltpu.CompilerParams(vmem_limit_bytes=VMEM_LIMIT),
        cost_estimate=pl.CostEstimate(
            flops=4 * steps * columns * cells, transcendentals=0, bytes_accessed=16 * 1024 * 1024
        ),
        name="gradients",
    )(slots, near, low, own, high)


def payload_kernel(where, low, own, high, target, held, sems):
    count, columns, cells = own.shape
    width = low.shape[0]

    def each(act):
        for i in range(5):
            index = where[i]

            @pl.when(index < width)
            def from_low():
                act(pltpu.make_async_copy(low.at[index], held.at[i], sems.at[i]))

            @pl.when((index >= width) & (index < width + count))
            def from_own():
                act(pltpu.make_async_copy(own.at[index - width], held.at[i], sems.at[i]))

            @pl.when(index >= width + count)
            def from_high():
                act(pltpu.make_async_copy(high.at[index - width - count], held.at[i], sems.at[i]))

    each(lambda copy: copy.start())
    each(lambda copy: copy.wait())
    target[0, :, :cells] = held[0]
    for axis in range(2):
        for begin in range(0, columns, 128):
            rows = pl.ds(begin, 128)
            a = held[1 + 2 * axis, rows, :].astype(jnp.float32)
            b = held[2 + 2 * axis, rows, :].astype(jnp.float32)
            target[0, rows, (axis + 1) * cells : (axis + 2) * cells] = (0.5 * (a - b)).astype(
                target.dtype
            )


def one_payload(where, low, own, high):
    count, columns, cells = own.shape
    return pl.pallas_call(
        payload_kernel,
        out_shape=jax.ShapeDtypeStruct((1, columns, 3 * cells), own.dtype),
        in_specs=[smem_spec()] + [any_spec()] * 3,
        out_specs=pl.BlockSpec(memory_space=pltpu.VMEM),
        scratch_shapes=[
            pltpu.VMEM((5, columns, cells), own.dtype),
            pltpu.SemaphoreType.DMA((5,)),
        ],
        cost_estimate=pl.CostEstimate(flops=0, transcendentals=0, bytes_accessed=1024 * 1024),
        name="payload",
    )(where, low, own, high)


def remap_kernel(first_row, depth_k, has_total, final, plan, *refs):
    if has_total:
        total_in, received, weights, out, total, fields, tiles, order, sems, total_sem = refs
    else:
        received, weights, out, total, fields, tiles, order, sems, total_sem = refs
    sources = received.shape[0]
    columns = total.shape[1]
    cells = weights.shape[2]

    def note(q, live):
        order[live] = q
        return live + plan[q]

    live = lax.fori_loop(0, sources, note, 0)

    def copies(j):
        q = order[j]
        place = lax.rem(j, DEPTH)
        first = lax.shift_right_logical(plan[sources + q], 3)
        second = lax.shift_right_logical(plan[2 * sources + q], 3)
        rows = pl.ds(first_row, depth_k)
        return (
            pltpu.make_async_copy(
                received.at[q, pl.ds(0, columns)], fields.at[place], sems.at[0, place]
            ),
            pltpu.make_async_copy(
                weights.at[first, rows], tiles.at[place, :, pl.ds(0, cells)], sems.at[1, place]
            ),
            pltpu.make_async_copy(
                weights.at[second, rows], tiles.at[place, :, pl.ds(cells, cells)], sems.at[2, place]
            ),
        )

    def start(j, carry):
        for copy in copies(j):
            copy.start()
        return carry

    lax.fori_loop(0, jnp.minimum(live, DEPTH), start, 0)
    if has_total:
        copy = pltpu.make_async_copy(total_in, total, total_sem.at[0])
        copy.start()
        copy.wait()
    else:
        total[...] = jnp.zeros_like(total)

    part = min(columns, 256)

    def add(j, carry):
        for copy in copies(j):
            copy.wait()
        q = order[j]
        place = lax.rem(j, DEPTH)
        first_ocean = plan[sources + q] & 7
        second_ocean = plan[2 * sources + q] & 7
        for begin in range(0, columns, part):
            rows = pl.ds(begin, part)
            product = jnp.dot(
                fields[place, rows, :], tiles[place], preferred_element_type=jnp.float32
            )
            total[first_ocean, rows, :] += product[:, :cells]
            total[second_ocean, rows, :] += product[:, cells:]

        @pl.when(j + DEPTH < live)
        def more():
            start(j + DEPTH, 0)

        return carry

    lax.fori_loop(0, live, add, 0)
    out[...] = total[...].astype(out.dtype)


def remap(plan, received, weights, total, first_row, ocean_count, columns, final):
    sources, unused, depth_k = received.shape
    cells = weights.shape[2]
    shape = (ocean_count, columns, cells)
    whole = pl.BlockSpec(memory_space=pltpu.VMEM)
    has_total = total is not None
    kernel = functools.partial(remap_kernel, first_row, depth_k, has_total, final)
    return pl.pallas_call(
        kernel,
        out_shape=jax.ShapeDtypeStruct(shape, jnp.bfloat16 if final else jnp.float32),
        in_specs=[smem_spec()] + [any_spec()] * has_total + [any_spec(), any_spec()],
        out_specs=whole,
        scratch_shapes=[
            pltpu.VMEM(shape, jnp.float32),
            pltpu.VMEM((DEPTH, columns, depth_k), received.dtype),
            pltpu.VMEM((DEPTH, depth_k, 2 * cells), weights.dtype),
            pltpu.SMEM((sources + 1,), jnp.int32),
            pltpu.SemaphoreType.DMA((3, DEPTH)),
            pltpu.SemaphoreType.DMA((1,)),
        ],
        compiler_params=pltpu.CompilerParams(vmem_limit_bytes=VMEM_LIMIT),
        cost_estimate=pl.CostEstimate(
            flops=4 * sources * columns * depth_k * cells,
            transcendentals=0,
            bytes_accessed=2 * sources * columns * depth_k * 2,
        ),
        name="remap",
    )(plan, *([total] if has_total else []), received, weights)


def body(atm_fields, neighbours, send_slots, send_counts, tile_weights, tile_rows, tile_cols):
    block_count, column_count, cell_count = atm_fields.shape
    peers = lax.axis_size("gy")
    ocean_count = block_count // 4
    tile_count = tile_weights.shape[0]
    halo_width = block_count // 4
    slots = send_slots.reshape(peers, -1)
    own_counts = send_counts.reshape(peers)
    me = lax.axis_index("gy")

    def exchange(blocks):
        return lax.all_to_all(blocks, "gy", split_axis=0, concat_axis=0, tiled=True)

    doubled = own_counts >= 2
    before = jnp.cumsum(doubled.astype(jnp.int32))
    overflow = jnp.sum(jnp.where(doubled & (before == 1), slots[:, 1], 0))
    low, high = neighbour_blocks(atm_fields, halo_width)
    facts = jnp.stack([own_counts, before, jnp.broadcast_to(before[-1], before.shape)], axis=1)
    note = jnp.pad(facts.astype(atm_fields.dtype), ((0, 0), (0, cell_count - 3)))
    near = neighbours - (lax.axis_index(("gx", "gy")) * block_count - halo_width)
    where = jnp.concatenate([overflow[None] + halo_width, near[overflow]])
    near = near.reshape(-1)
    values = exchange(in_order(atm_fields, slots[:, 0], note))
    spares = lax.all_gather(
        one_payload(where, low, atm_fields, high), "gy", axis=0, tiled=True
    )
    slopes = gradients(slots[:, 0], near, low, atm_fields, high)
    slopes, values = lax.optimization_barrier((slopes, values))
    slopes = exchange(slopes)

    told = values[:, column_count, :3].astype(jnp.int32)
    arrived, rank = told[:, 0], told[:, 1]
    most = jnp.max(told[:, 2])
    planes = lax.axis_size("gx")
    ahead = [
        lax.ppermute(most, "gx", [(i, (i + step) % planes) for i in range(planes)])
        for step in range(1, planes)
    ]
    for other in ahead:
        most = jnp.maximum(most, other)
    slot_ids = lax.broadcasted_iota(jnp.int32, (2 * peers, tile_count), 0)
    codes = lax.broadcasted_iota(jnp.int32, (2 * peers, tile_count), 1) * 8 + tile_rows[None, :]
    named = slot_ids == tile_cols[None, :]
    first_code = jnp.min(jnp.where(named, codes, 8 * tile_count), axis=1).reshape(peers, 2)
    second_code = jnp.max(jnp.where(named, codes, -1), axis=1).reshape(peers, 2)

    def plan(live, slot):
        return jnp.concatenate([live.astype(jnp.int32), first_code[:, slot], second_code[:, slot]])

    plan_first = plan(arrived >= 1, 0)
    plan_spare = plan((arrived >= 2) & (rank == 1), 1)
    plan_rest = plan((arrived >= 2) & (rank > 1), 1)

    def add(this_plan, received, total, first_row, final=False):
        return remap(
            this_plan, received, tile_weights, total, first_row, ocean_count, column_count, final
        )

    total = add(plan_first, values, None, 0)
    total = add(plan_spare, spares, total, 0)

    def finish(total):
        return add(plan_first, slopes, total, cell_count, final=True)

    def with_rest(total, unused):
        rest_slopes = gradients(slots[:, 1], near, low, atm_fields, high)
        total = add(plan_rest, exchange(in_order(atm_fields, slots[:, 1], note)), total, 0)
        return finish(add(plan_rest, exchange(rest_slopes), total, cell_count))

    return lax.cond(most > 1, with_rest, lambda unused, done: done, total, finish(total))


def solution(mesh):
    return jax.shard_map(
        body,
        mesh=mesh,
        in_specs=(
            P(("gx", "gy"), None, None),
            P(("gx", "gy"), None),
            P(("gx", "gy"), None, None),
            P(("gx", "gy"), None),
            P(("gx", "gy"), None, None),
            P(("gx", "gy")),
            P(("gx", "gy")),
        ),
        out_specs=P(("gx", "gy"), None, None),
        check_vma=False,
    )
```

```python
import functools

import jax
import jax.numpy as jnp
from jax import lax
from jax.experimental import pallas as pl
from jax.experimental.pallas import tpu as pltpu
from jax.sharding import PartitionSpec as P

VMEM_LIMIT = 58 * 1024 * 1024
DEPTH = 8
GROUPS = 4
NOTE = 16


def any_spec():
    return pl.BlockSpec(memory_space=pl.ANY)


def hbm_spec():
    return pl.BlockSpec(memory_space=pltpu.HBM)


def smem_spec():
    return pl.BlockSpec(memory_space=pltpu.SMEM)


def neighbour_blocks(block, width):
    axes = ("gx", "gy")
    count = lax.axis_size(axes)
    forward = [(i, i + 1) for i in range(count - 1)]
    backward = [(target, source) for source, target in forward]
    low = lax.ppermute(block[-width:], axes, forward)
    high = lax.ppermute(block[:width], axes, backward)
    return low, high


def order_kernel(slots, note, source, target, held, sems):
    count = target.shape[0]
    columns = source.shape[1]
    held[:, columns:, :] = jnp.broadcast_to(note[...][:, None, :], (count, NOTE, note.shape[1]))

    def fetch(i):
        return pltpu.make_async_copy(
            source.at[slots[i]], held.at[i, pl.ds(0, columns)], sems.at[0, i]
        )

    def store(i):
        return pltpu.make_async_copy(held.at[i], target.at[i], sems.at[1, i])

    def begin(i, carry):
        fetch(i).start()
        return carry

    def turn(i, carry):
        fetch(i).wait()
        store(i).start()
        return carry

    def end(i, carry):
        store(i).wait()
        return carry

    lax.fori_loop(0, count, begin, 0)
    lax.fori_loop(0, count, turn, 0)
    lax.fori_loop(0, count, end, 0)


def in_order(blocks, slots, note):
    count = slots.shape[0]
    shape = (count, blocks.shape[1] + NOTE, blocks.shape[2])
    return pl.pallas_call(
        order_kernel,
        out_shape=pltpu.HBM(shape, blocks.dtype),
        in_specs=[smem_spec(), pl.BlockSpec(memory_space=pltpu.VMEM), any_spec()],
        out_specs=hbm_spec(),
        scratch_shapes=[
            pltpu.VMEM(shape, blocks.dtype),
            pltpu.SemaphoreType.DMA((2, count)),
        ],
        compiler_params=pltpu.CompilerParams(vmem_limit_bytes=VMEM_LIMIT),
        cost_estimate=pl.CostEstimate(
            flops=0, transcendentals=0, bytes_accessed=4 * count * shape[1] * shape[2]
        ),
        name="order",
    )(slots, note, blocks)


def gradient_kernel(slots, near, low, own, high, target, held, made, sems, out_sems):
    count, columns, cells = own.shape
    width = low.shape[0]
    steps = target.shape[0]
    copies = [
        pltpu.make_async_copy(low, held.at[pl.ds(0, width)], sems.at[0]),
        pltpu.make_async_copy(own, held.at[pl.ds(width, count)], sems.at[1]),
        pltpu.make_async_copy(high, held.at[pl.ds(width + count, width)], sems.at[2]),
    ]
    for copy in copies:
        copy.start()
    for copy in copies:
        copy.wait()

    def make(i):
        block = slots[i]
        for axis in range(2):
            first = near[4 * block + 2 * axis]
            second = near[4 * block + 2 * axis + 1]
            for begin in range(0, columns, 128):
                rows = pl.ds(begin, 128)
                a = held[first, rows, :].astype(jnp.float32)
                b = held[second, rows, :].astype(jnp.float32)
                made[i, rows, axis * cells : (axis + 1) * cells] = (0.5 * (a - b)).astype(made.dtype)

    def store(i):
        return pltpu.make_async_copy(made.at[i], target.at[i], out_sems.at[i])

    def turn(i, carry):
        make(i)
        store(i).start()
        return carry

    def end(i, carry):
        store(i).wait()
        return carry

    lax.fori_loop(0, steps, turn, 0)
    lax.fori_loop(0, steps, end, 0)


def gradients(slots, near, low, own, high):
    width = low.shape[0]
    count, columns, cells = own.shape
    steps = slots.shape[0]
    return pl.pallas_call(
        gradient_kernel,
        out_shape=jax.ShapeDtypeStruct((steps, columns, 2 * cells), own.dtype),
        in_specs=[smem_spec(), smem_spec()] + [any_spec()] * 3,
        out_specs=any_spec(),
        scratch_shapes=[
            pltpu.VMEM((count + 2 * width, columns, cells), own.dtype),
            pltpu.VMEM((steps, columns, 2 * cells), own.dtype),
            pltpu.SemaphoreType.DMA((3,)),
            pltpu.SemaphoreType.DMA((steps,)),
        ],
        compiler_params=pltpu.CompilerParams(vmem_limit_bytes=VMEM_LIMIT),
        cost_estimate=pl.CostEstimate(
            flops=4 * steps * columns * cells, transcendentals=0, bytes_accessed=16 * 1024 * 1024
        ),
        name="gradients",
    )(slots, near, low, own, high)


def payload_kernel(where, low, own, high, target, held, sems):
    count, columns, cells = own.shape
    width = low.shape[0]

    def each(act):
        for i in range(5):
            index = where[i]

            @pl.when(index < width)
            def from_low():
                act(pltpu.make_async_copy(low.at[index], held.at[i], sems.at[i]))

            @pl.when((index >= width) & (index < width + count))
            def from_own():
                act(pltpu.make_async_copy(own.at[index - width], held.at[i], sems.at[i]))

            @pl.when(index >= width + count)
            def from_high():
                act(pltpu.make_async_copy(high.at[index - width - count], held.at[i], sems.at[i]))

    each(lambda copy: copy.start())
    each(lambda copy: copy.wait())
    target[0, :, :cells] = held[0]
    for axis in range(2):
        for begin in range(0, columns, 128):
            rows = pl.ds(begin, 128)
            a = held[1 + 2 * axis, rows, :].astype(jnp.float32)
            b = held[2 + 2 * axis, rows, :].astype(jnp.float32)
            target[0, rows, (axis + 1) * cells : (axis + 2) * cells] = (0.5 * (a - b)).astype(
                target.dtype
            )


def one_payload(where, low, own, high):
    count, columns, cells = own.shape
    return pl.pallas_call(
        payload_kernel,
        out_shape=jax.ShapeDtypeStruct((1, columns, 3 * cells), own.dtype),
        in_specs=[smem_spec()] + [any_spec()] * 3,
        out_specs=pl.BlockSpec(memory_space=pltpu.VMEM),
        scratch_shapes=[
            pltpu.VMEM((5, columns, cells), own.dtype),
            pltpu.SemaphoreType.DMA((5,)),
        ],
        cost_estimate=pl.CostEstimate(flops=0, transcendentals=0, bytes_accessed=1024 * 1024),
        name="payload",
    )(where, low, own, high)


def remap_kernel(first_row, depth_k, has_total, final, plan, *refs):
    if has_total:
        total_in, received, weights, out, total, fields, tiles, order, sems, total_sem = refs
    else:
        received, weights, out, total, fields, tiles, order, sems, total_sem = refs
    sources = received.shape[0]
    columns = total.shape[1]
    cells = weights.shape[2]

    def note(q, live):
        order[live] = q
        return live + plan[q]

    live = lax.fori_loop(0, sources, note, 0)

    def copies(j):
        q = order[j]
        place = lax.rem(j, DEPTH)
        first = lax.shift_right_logical(plan[sources + q], 3)
        second = lax.shift_right_logical(plan[2 * sources + q], 3)
        rows = pl.ds(first_row, depth_k)
        return (
            pltpu.make_async_copy(
                received.at[q, pl.ds(0, columns)], fields.at[place], sems.at[0, place]
            ),
            pltpu.make_async_copy(
                weights.at[first, rows], tiles.at[place, :, pl.ds(0, cells)], sems.at[1, place]
            ),
            pltpu.make_async_copy(
                weights.at[second, rows], tiles.at[place, :, pl.ds(cells, cells)], sems.at[2, place]
            ),
        )

    def start(j, carry):
        for copy in copies(j):
            copy.start()
        return carry

    lax.fori_loop(0, jnp.minimum(live, DEPTH), start, 0)
    if has_total:
        copy = pltpu.make_async_copy(total_in, total, total_sem.at[0])
        copy.start()
        copy.wait()
    else:
        total[...] = jnp.zeros_like(total)

    part = min(columns, 256)

    def add(j, carry):
        for copy in copies(j):
            copy.wait()
        q = order[j]
        place = lax.rem(j, DEPTH)
        first_ocean = plan[sources + q] & 7
        second_ocean = plan[2 * sources + q] & 7
        for begin in range(0, columns, part):
            rows = pl.ds(begin, part)
            product = jnp.dot(
                fields[place, rows, :], tiles[place], preferred_element_type=jnp.float32
            )
            total[first_ocean, rows, :] += product[:, :cells]
            total[second_ocean, rows, :] += product[:, cells:]

        @pl.when(j + DEPTH < live)
        def more():
            start(j + DEPTH, 0)

        return carry

    lax.fori_loop(0, live, add, 0)
    out[...] = total[...].astype(out.dtype)


def remap(plan, received, weights, total, first_row, ocean_count, columns, final):
    sources, unused, depth_k = received.shape
    cells = weights.shape[2]
    shape = (ocean_count, columns, cells)
    whole = pl.BlockSpec(memory_space=pltpu.VMEM)
    has_total = total is not None
    kernel = functools.partial(remap_kernel, first_row, depth_k, has_total, final)
    return pl.pallas_call(
        kernel,
        out_shape=jax.ShapeDtypeStruct(shape, jnp.bfloat16 if final else jnp.float32),
        in_specs=[smem_spec()] + [any_spec()] * has_total + [any_spec(), any_spec()],
        out_specs=whole,
        scratch_shapes=[
            pltpu.VMEM(shape, jnp.float32),
            pltpu.VMEM((DEPTH, columns, depth_k), received.dtype),
            pltpu.VMEM((DEPTH, depth_k, 2 * cells), weights.dtype),
            pltpu.SMEM((sources + 1,), jnp.int32),
            pltpu.SemaphoreType.DMA((3, DEPTH)),
            pltpu.SemaphoreType.DMA((1,)),
        ],
        compiler_params=pltpu.CompilerParams(vmem_limit_bytes=VMEM_LIMIT),
        cost_estimate=pl.CostEstimate(
            flops=4 * sources * columns * depth_k * cells,
            transcendentals=0,
            bytes_accessed=2 * sources * columns * depth_k * 2,
        ),
        name="remap",
    )(plan, *([total] if has_total else []), received, weights)


def pack_kernel(first_row, plan, weights, out, target, sems, out_sems):
    sources, depth_k, wide = target.shape
    cells = wide // 2
    rows = pl.ds(first_row, depth_k)

    def copies(q):
        return [
            pltpu.make_async_copy(
                weights.at[lax.shift_right_logical(plan[(1 + i) * sources + q], 3), rows],
                target.at[q, :, pl.ds(i * cells, cells)],
                sems.at[i, q],
            )
            for i in range(2)
        ]

    def start(q, carry):
        for copy in copies(q):
            copy.start()
        return carry

    def end(q, carry):
        for copy in copies(q):
            copy.wait()

        @pl.when(plan[q] == 0)
        def dead():
            target[q] = jnp.zeros_like(target[q])

        store(q).start()
        return carry

    def store(q):
        return pltpu.make_async_copy(target.at[q], out.at[q], out_sems.at[q])

    def finish(q, carry):
        store(q).wait()
        return carry

    lax.fori_loop(0, sources, start, 0)
    lax.fori_loop(0, sources, end, 0)
    lax.fori_loop(0, sources, finish, 0)


def pack(plan, weights, first_row, depth_k):
    sources = plan.shape[0] // 3
    cells = weights.shape[2]
    return pl.pallas_call(
        functools.partial(pack_kernel, first_row),
        out_shape=pltpu.HBM((sources, depth_k, 2 * cells), weights.dtype),
        in_specs=[smem_spec(), hbm_spec()],
        out_specs=hbm_spec(),
        scratch_shapes=[
            pltpu.VMEM((sources, depth_k, 2 * cells), weights.dtype),
            pltpu.SemaphoreType.DMA((2, sources)),
            pltpu.SemaphoreType.DMA((sources,)),
        ],
        compiler_params=pltpu.CompilerParams(vmem_limit_bytes=VMEM_LIMIT),
        cost_estimate=pl.CostEstimate(
            flops=0, transcendentals=0, bytes_accessed=8 * sources * depth_k * cells
        ),
        name="pack",
    )(plan, weights)


def packed_kernel(has_total, plan, *refs):
    if has_total:
        total_in, tiles, received, out, total, held, fields, rounded, sems, total_sems = refs
    else:
        tiles, received, out, total, held, fields, rounded, sems, total_sems = refs
    sources, columns, depth_k = received.shape
    oceans, unused, cells = out.shape
    group = sources // GROUPS

    def fetch(g):
        some = pl.ds(g * group, group)
        return (
            pltpu.make_async_copy(received.at[some], fields.at[some], sems.at[0, g]),
            pltpu.make_async_copy(tiles.at[some], held.at[some], sems.at[1, g]),
        )

    live = lax.fori_loop(0, sources, lambda q, seen: seen + plan[q], 0)
    if has_total:
        earlier = pltpu.make_async_copy(total_in, total, total_sems.at[0])
        earlier.start()

    @pl.when(live > 0)
    def begin():
        for g in range(GROUPS):
            for copy in fetch(g):
                copy.start()

    if has_total:
        earlier.wait()
    else:
        total[...] = jnp.zeros_like(total)
    part = min(columns, 256)

    def add(q, carry):
        first_ocean = plan[sources + q] & 7
        second_ocean = plan[2 * sources + q] & 7
        for begin in range(0, columns, part):
            rows = pl.ds(begin, part)
            product = jnp.dot(fields[q, rows, :], held[q], preferred_element_type=jnp.float32)
            total[first_ocean, rows, :] += product[:, :cells]
            total[second_ocean, rows, :] += product[:, cells:]
        return carry

    @pl.when(live > 0)
    def work():
        for g in range(GROUPS):
            for copy in fetch(g):
                copy.wait()
            lax.fori_loop(g * group, (g + 1) * group, add, 0, unroll=group)

    stores = []
    for o in range(oceans):
        source = total
        if out.dtype != total.dtype:
            rounded[o] = total[o].astype(out.dtype)
            source = rounded
        store = pltpu.make_async_copy(source.at[o], out.at[o], total_sems.at[o])
        store.start()
        stores.append(store)
    for store in stores:
        store.wait()


def remap_packed(plan, total, tiles, received, ocean_count, dtype):
    sources, columns, depth_k = received.shape
    shape = (ocean_count, columns, tiles.shape[2] // 2)
    has_total = total is not None
    return pl.pallas_call(
        functools.partial(packed_kernel, has_total),
        out_shape=pltpu.HBM(shape, dtype),
        in_specs=[smem_spec()] + [hbm_spec()] * (2 + has_total),
        out_specs=hbm_spec(),
        scratch_shapes=[
            pltpu.VMEM(shape, jnp.float32),
            pltpu.VMEM(tiles.shape, tiles.dtype),
            pltpu.VMEM(received.shape, received.dtype),
            pltpu.VMEM(shape, jnp.bfloat16),
            pltpu.SemaphoreType.DMA((2, GROUPS)),
            pltpu.SemaphoreType.DMA((ocean_count,)),
        ],
        compiler_params=pltpu.CompilerParams(vmem_limit_bytes=VMEM_LIMIT),
        cost_estimate=pl.CostEstimate(
            flops=4 * sources * columns * depth_k * shape[2],
            transcendentals=0,
            bytes_accessed=2 * sources * columns * depth_k,
        ),
        name="remap_packed",
    )(plan, *([total] if has_total else []), tiles, received)


def body(atm_fields, neighbours, send_slots, send_counts, tile_weights, tile_rows, tile_cols):
    block_count, column_count, cell_count = atm_fields.shape
    peers = lax.axis_size("gy")
    ocean_count = block_count // 4
    tile_count = tile_weights.shape[0]
    halo_width = block_count // 4
    slots = send_slots.reshape(peers, -1)
    own_counts = send_counts.reshape(peers)
    me = lax.axis_index("gy")

    def exchange(blocks):
        return lax.all_to_all(blocks, "gy", split_axis=0, concat_axis=0, tiled=True)

    doubled = own_counts >= 2
    before = jnp.cumsum(doubled.astype(jnp.int32))
    overflow = jnp.sum(jnp.where(doubled & (before == 1), slots[:, 1], 0))
    low, high = neighbour_blocks(atm_fields, halo_width)
    facts = jnp.stack([own_counts, before, jnp.broadcast_to(before[-1], before.shape)], axis=1)
    note = jnp.pad(facts.astype(atm_fields.dtype), ((0, 0), (0, cell_count - 3)))
    near = neighbours - (lax.axis_index(("gx", "gy")) * block_count - halo_width)
    where = jnp.concatenate([overflow[None] + halo_width, near[overflow]])
    near = near.reshape(-1)
    values = exchange(in_order(atm_fields, slots[:, 0], note))
    spares = lax.all_gather(
        one_payload(where, low, atm_fields, high), "gy", axis=0, tiled=True
    )
    slopes = gradients(slots[:, 0], near, low, atm_fields, high)
    slopes, values = lax.optimization_barrier((slopes, values))
    slopes = exchange(slopes)

    told = values[:, column_count, :3].astype(jnp.int32)
    arrived, rank = told[:, 0], told[:, 1]
    most = jnp.max(told[:, 2])
    planes = lax.axis_size("gx")
    ahead = [
        lax.ppermute(most, "gx", [(i, (i + step) % planes) for i in range(planes)])
        for step in range(1, planes)
    ]
    for other in ahead:
        most = jnp.maximum(most, other)
    slot_ids = lax.broadcasted_iota(jnp.int32, (2 * peers, tile_count), 0)
    codes = lax.broadcasted_iota(jnp.int32, (2 * peers, tile_count), 1) * 8 + tile_rows[None, :]
    named = slot_ids == tile_cols[None, :]
    first_code = jnp.min(jnp.where(named, codes, 8 * tile_count), axis=1).reshape(peers, 2)
    second_code = jnp.max(jnp.where(named, codes, -1), axis=1).reshape(peers, 2)

    def plan(live, slot):
        return jnp.concatenate([live.astype(jnp.int32), first_code[:, slot], second_code[:, slot]])

    plan_first = plan(arrived >= 1, 0)
    plan_spare = plan((arrived >= 2) & (rank == 1), 1)
    plan_rest = plan((arrived >= 2) & (rank > 1), 1)

    def add(this_plan, received, total, first_row, final=False):
        return remap(
            this_plan, received, tile_weights, total, first_row, ocean_count, column_count, final
        )

    total = add(plan_first, values, None, 0)
    total = add(plan_spare, spares, total, 0)

    tiles = pack(plan_first, tile_weights, cell_count, 2 * cell_count)
    done = remap_packed(plan_first, total, tiles, slopes, ocean_count, jnp.bfloat16)

    def with_rest(total, unused):
        rest_slopes = gradients(slots[:, 1], near, low, atm_fields, high)
        total = add(plan_rest, exchange(in_order(atm_fields, slots[:, 1], note)), total, 0)
        total = add(plan_rest, exchange(rest_slopes), total, cell_count)
        return add(plan_first, slopes, total, cell_count, final=True)

    return lax.cond(most > 1, with_rest, lambda unused, done: done, total, done)


def solution(mesh):
    return jax.shard_map(
        body,
        mesh=mesh,
        in_specs=(
            P(("gx", "gy"), None, None),
            P(("gx", "gy"), None),
            P(("gx", "gy"), None, None),
            P(("gx", "gy"), None),
            P(("gx", "gy"), None, None),
            P(("gx", "gy")),
            P(("gx", "gy")),
        ),
        out_specs=P(("gx", "gy"), None, None),
        check_vma=False,
    )
```

```python
import functools

import jax
import jax.numpy as jnp
from jax import lax
from jax.experimental import pallas as pl
from jax.experimental.pallas import tpu as pltpu
from jax.sharding import PartitionSpec as P

VMEM_LIMIT = 58 * 1024 * 1024
DEPTH = 8
GROUP_ENDS = (0, 1, 4, 8, 12, 16)
GROUPS = len(GROUP_ENDS) - 1
NOTE = 16


def any_spec():
    return pl.BlockSpec(memory_space=pl.ANY)


def hbm_spec():
    return pl.BlockSpec(memory_space=pltpu.HBM)


def smem_spec():
    return pl.BlockSpec(memory_space=pltpu.SMEM)


def neighbour_blocks(block, width):
    axes = ("gx", "gy")
    count = lax.axis_size(axes)
    forward = [(i, i + 1) for i in range(count - 1)]
    backward = [(target, source) for source, target in forward]
    low = lax.ppermute(block[-width:], axes, forward)
    high = lax.ppermute(block[:width], axes, backward)
    return low, high


def order_kernel(slots, note, source, target, held, sems):
    count = target.shape[0]
    columns = source.shape[1]
    held[:, columns:, :] = jnp.broadcast_to(note[...][:, None, :], (count, NOTE, note.shape[1]))

    def fetch(i):
        return pltpu.make_async_copy(
            source.at[slots[i]], held.at[i, pl.ds(0, columns)], sems.at[0, i]
        )

    def store(i):
        return pltpu.make_async_copy(held.at[i], target.at[i], sems.at[1, i])

    def begin(i, carry):
        fetch(i).start()
        return carry

    def turn(i, carry):
        fetch(i).wait()
        store(i).start()
        return carry

    def end(i, carry):
        store(i).wait()
        return carry

    lax.fori_loop(0, count, begin, 0)
    lax.fori_loop(0, count, turn, 0)
    lax.fori_loop(0, count, end, 0)


def in_order(blocks, slots, note):
    count = slots.shape[0]
    shape = (count, blocks.shape[1] + NOTE, blocks.shape[2])
    return pl.pallas_call(
        order_kernel,
        out_shape=pltpu.HBM(shape, blocks.dtype),
        in_specs=[smem_spec(), pl.BlockSpec(memory_space=pltpu.VMEM), any_spec()],
        out_specs=hbm_spec(),
        scratch_shapes=[
            pltpu.VMEM(shape, blocks.dtype),
            pltpu.SemaphoreType.DMA((2, count)),
        ],
        compiler_params=pltpu.CompilerParams(vmem_limit_bytes=VMEM_LIMIT),
        cost_estimate=pl.CostEstimate(
            flops=0, transcendentals=0, bytes_accessed=4 * count * shape[1] * shape[2]
        ),
        name="order",
    )(slots, note, blocks)


def gradient_kernel(slots, near, low, own, high, target, held, made, sems, out_sems):
    count, columns, cells = own.shape
    width = low.shape[0]
    steps = target.shape[0]
    copies = [
        pltpu.make_async_copy(low, held.at[pl.ds(0, width)], sems.at[0]),
        pltpu.make_async_copy(own, held.at[pl.ds(width, count)], sems.at[1]),
        pltpu.make_async_copy(high, held.at[pl.ds(width + count, width)], sems.at[2]),
    ]
    for copy in copies:
        copy.start()
    for copy in copies:
        copy.wait()

    def make(i):
        block = slots[i]
        for axis in range(2):
            first = near[4 * block + 2 * axis]
            second = near[4 * block + 2 * axis + 1]
            for begin in range(0, columns, 128):
                rows = pl.ds(begin, 128)
                a = held[first, rows, :].astype(jnp.float32)
                b = held[second, rows, :].astype(jnp.float32)
                made[i, rows, axis * cells : (axis + 1) * cells] = (0.5 * (a - b)).astype(made.dtype)

    def store(i):
        return pltpu.make_async_copy(made.at[i], target.at[i], out_sems.at[i])

    def turn(i, carry):
        make(i)
        store(i).start()
        return carry

    def end(i, carry):
        store(i).wait()
        return carry

    lax.fori_loop(0, steps, turn, 0)
    lax.fori_loop(0, steps, end, 0)


def gradients(slots, near, low, own, high):
    width = low.shape[0]
    count, columns, cells = own.shape
    steps = slots.shape[0]
    return pl.pallas_call(
        gradient_kernel,
        out_shape=jax.ShapeDtypeStruct((steps, columns, 2 * cells), own.dtype),
        in_specs=[smem_spec(), smem_spec()] + [any_spec()] * 3,
        out_specs=any_spec(),
        scratch_shapes=[
            pltpu.VMEM((count + 2 * width, columns, cells), own.dtype),
            pltpu.VMEM((steps, columns, 2 * cells), own.dtype),
            pltpu.SemaphoreType.DMA((3,)),
            pltpu.SemaphoreType.DMA((steps,)),
        ],
        compiler_params=pltpu.CompilerParams(vmem_limit_bytes=VMEM_LIMIT),
        cost_estimate=pl.CostEstimate(
            flops=4 * steps * columns * cells, transcendentals=0, bytes_accessed=16 * 1024 * 1024
        ),
        name="gradients",
    )(slots, near, low, own, high)


def payload_kernel(where, low, own, high, target, held, sems):
    count, columns, cells = own.shape
    width = low.shape[0]

    def each(act):
        for i in range(5):
            index = where[i]

            @pl.when(index < width)
            def from_low():
                act(pltpu.make_async_copy(low.at[index], held.at[i], sems.at[i]))

            @pl.when((index >= width) & (index < width + count))
            def from_own():
                act(pltpu.make_async_copy(own.at[index - width], held.at[i], sems.at[i]))

            @pl.when(index >= width + count)
            def from_high():
                act(pltpu.make_async_copy(high.at[index - width - count], held.at[i], sems.at[i]))

    each(lambda copy: copy.start())
    each(lambda copy: copy.wait())
    target[0, :, :cells] = held[0]
    for axis in range(2):
        for begin in range(0, columns, 128):
            rows = pl.ds(begin, 128)
            a = held[1 + 2 * axis, rows, :].astype(jnp.float32)
            b = held[2 + 2 * axis, rows, :].astype(jnp.float32)
            target[0, rows, (axis + 1) * cells : (axis + 2) * cells] = (0.5 * (a - b)).astype(
                target.dtype
            )


def one_payload(where, low, own, high):
    count, columns, cells = own.shape
    return pl.pallas_call(
        payload_kernel,
        out_shape=jax.ShapeDtypeStruct((1, columns, 3 * cells), own.dtype),
        in_specs=[smem_spec()] + [any_spec()] * 3,
        out_specs=pl.BlockSpec(memory_space=pltpu.VMEM),
        scratch_shapes=[
            pltpu.VMEM((5, columns, cells), own.dtype),
            pltpu.SemaphoreType.DMA((5,)),
        ],
        cost_estimate=pl.CostEstimate(flops=0, transcendentals=0, bytes_accessed=1024 * 1024),
        name="payload",
    )(where, low, own, high)


def remap_kernel(first_row, depth_k, has_total, final, plan, *refs):
    if has_total:
        total_in, received, weights, out, total, fields, tiles, order, sems, total_sem = refs
    else:
        received, weights, out, total, fields, tiles, order, sems, total_sem = refs
    sources = received.shape[0]
    columns = total.shape[1]
    cells = weights.shape[2]

    def note(q, live):
        order[live] = q
        return live + plan[q]

    live = lax.fori_loop(0, sources, note, 0)

    def copies(j):
        q = order[j]
        place = lax.rem(j, DEPTH)
        first = lax.shift_right_logical(plan[sources + q], 3)
        second = lax.shift_right_logical(plan[2 * sources + q], 3)
        rows = pl.ds(first_row, depth_k)
        return (
            pltpu.make_async_copy(
                received.at[q, pl.ds(0, columns)], fields.at[place], sems.at[0, place]
            ),
            pltpu.make_async_copy(
                weights.at[first, rows], tiles.at[place, :, pl.ds(0, cells)], sems.at[1, place]
            ),
            pltpu.make_async_copy(
                weights.at[second, rows], tiles.at[place, :, pl.ds(cells, cells)], sems.at[2, place]
            ),
        )

    def start(j, carry):
        for copy in copies(j):
            copy.start()
        return carry

    lax.fori_loop(0, jnp.minimum(live, DEPTH), start, 0)
    if has_total:
        copy = pltpu.make_async_copy(total_in, total, total_sem.at[0])
        copy.start()
        copy.wait()
    else:
        total[...] = jnp.zeros_like(total)

    part = min(columns, 256)

    def add(j, carry):
        for copy in copies(j):
            copy.wait()
        q = order[j]
        place = lax.rem(j, DEPTH)
        first_ocean = plan[sources + q] & 7
        second_ocean = plan[2 * sources + q] & 7
        for begin in range(0, columns, part):
            rows = pl.ds(begin, part)
            product = jnp.dot(
                fields[place, rows, :], tiles[place], preferred_element_type=jnp.float32
            )
            total[first_ocean, rows, :] += product[:, :cells]
            total[second_ocean, rows, :] += product[:, cells:]

        @pl.when(j + DEPTH < live)
        def more():
            start(j + DEPTH, 0)

        return carry

    lax.fori_loop(0, live, add, 0)
    out[...] = total[...].astype(out.dtype)


def remap(plan, received, weights, total, first_row, ocean_count, columns, final):
    sources, unused, depth_k = received.shape
    cells = weights.shape[2]
    shape = (ocean_count, columns, cells)
    whole = pl.BlockSpec(memory_space=pltpu.VMEM)
    has_total = total is not None
    kernel = functools.partial(remap_kernel, first_row, depth_k, has_total, final)
    return pl.pallas_call(
        kernel,
        out_shape=jax.ShapeDtypeStruct(shape, jnp.bfloat16 if final else jnp.float32),
        in_specs=[smem_spec()] + [any_spec()] * has_total + [any_spec(), any_spec()],
        out_specs=whole,
        scratch_shapes=[
            pltpu.VMEM(shape, jnp.float32),
            pltpu.VMEM((DEPTH, columns, depth_k), received.dtype),
            pltpu.VMEM((DEPTH, depth_k, 2 * cells), weights.dtype),
            pltpu.SMEM((sources + 1,), jnp.int32),
            pltpu.SemaphoreType.DMA((3, DEPTH)),
            pltpu.SemaphoreType.DMA((1,)),
        ],
        compiler_params=pltpu.CompilerParams(vmem_limit_bytes=VMEM_LIMIT),
        cost_estimate=pl.CostEstimate(
            flops=4 * sources * columns * depth_k * cells,
            transcendentals=0,
            bytes_accessed=2 * sources * columns * depth_k * 2,
        ),
        name="remap",
    )(plan, *([total] if has_total else []), received, weights)


def pack_kernel(first_row, plan, weights, out, target, sems, out_sems):
    sources, depth_k, wide = target.shape
    cells = wide // 2
    rows = pl.ds(first_row, depth_k)

    def copies(q):
        return [
            pltpu.make_async_copy(
                weights.at[lax.shift_right_logical(plan[(1 + i) * sources + q], 3), rows],
                target.at[q, :, pl.ds(i * cells, cells)],
                sems.at[i, q],
            )
            for i in range(2)
        ]

    def start(q, carry):
        for copy in copies(q):
            copy.start()
        return carry

    def end(q, carry):
        for copy in copies(q):
            copy.wait()

        @pl.when(plan[q] == 0)
        def dead():
            target[q] = jnp.zeros_like(target[q])

        store(q).start()
        return carry

    def store(q):
        return pltpu.make_async_copy(target.at[q], out.at[q], out_sems.at[q])

    def finish(q, carry):
        store(q).wait()
        return carry

    lax.fori_loop(0, sources, start, 0)
    lax.fori_loop(0, sources, end, 0)
    lax.fori_loop(0, sources, finish, 0)


def pack(plan, weights, first_row, depth_k):
    sources = plan.shape[0] // 3
    cells = weights.shape[2]
    return pl.pallas_call(
        functools.partial(pack_kernel, first_row),
        out_shape=pltpu.HBM((sources, depth_k, 2 * cells), weights.dtype),
        in_specs=[smem_spec(), hbm_spec()],
        out_specs=hbm_spec(),
        scratch_shapes=[
            pltpu.VMEM((sources, depth_k, 2 * cells), weights.dtype),
            pltpu.SemaphoreType.DMA((2, sources)),
            pltpu.SemaphoreType.DMA((sources,)),
        ],
        compiler_params=pltpu.CompilerParams(vmem_limit_bytes=VMEM_LIMIT),
        cost_estimate=pl.CostEstimate(
            flops=0, transcendentals=0, bytes_accessed=8 * sources * depth_k * cells
        ),
        name="pack",
    )(plan, weights)


def packed_kernel(has_total, plan, *refs):
    if has_total:
        total_in, tiles, received, out, total, held, fields, rounded, sems, total_sems = refs
    else:
        tiles, received, out, total, held, fields, rounded, sems, total_sems = refs
    sources, columns, depth_k = received.shape
    oceans, unused, cells = out.shape
    ends = [end * sources // 16 for end in GROUP_ENDS]

    def fetch(g):
        some = pl.ds(ends[g], ends[g + 1] - ends[g])
        return (
            pltpu.make_async_copy(received.at[some], fields.at[some], sems.at[0, g]),
            pltpu.make_async_copy(tiles.at[some], held.at[some], sems.at[1, g]),
        )

    live = lax.fori_loop(0, sources, lambda q, seen: seen + plan[q], 0)
    if has_total:
        earlier = pltpu.make_async_copy(total_in, total, total_sems.at[0])
        earlier.start()

    @pl.when(live > 0)
    def begin():
        for g in range(GROUPS):
            for copy in fetch(g):
                copy.start()

    if has_total:
        earlier.wait()
    else:
        total[...] = jnp.zeros_like(total)
    part = min(columns, 256)

    def add(q, carry):
        first_ocean = plan[sources + q] & 7
        second_ocean = plan[2 * sources + q] & 7
        for begin in range(0, columns, part):
            rows = pl.ds(begin, part)
            product = jnp.dot(fields[q, rows, :], held[q], preferred_element_type=jnp.float32)
            total[first_ocean, rows, :] += product[:, :cells]
            total[second_ocean, rows, :] += product[:, cells:]
        return carry

    @pl.when(live > 0)
    def work():
        for g in range(GROUPS):
            for copy in fetch(g):
                copy.wait()
            lax.fori_loop(ends[g], ends[g + 1], add, 0, unroll=ends[g + 1] - ends[g])

    stores = []
    for o in range(oceans):
        source = total
        if out.dtype != total.dtype:
            rounded[o] = total[o].astype(out.dtype)
            source = rounded
        store = pltpu.make_async_copy(source.at[o], out.at[o], total_sems.at[o])
        store.start()
        stores.append(store)
    for store in stores:
        store.wait()


def remap_packed(plan, total, tiles, received, ocean_count, dtype):
    sources, columns, depth_k = received.shape
    shape = (ocean_count, columns, tiles.shape[2] // 2)
    has_total = total is not None
    return pl.pallas_call(
        functools.partial(packed_kernel, has_total),
        out_shape=pltpu.HBM(shape, dtype),
        in_specs=[smem_spec()] + [hbm_spec()] * (2 + has_total),
        out_specs=hbm_spec(),
        scratch_shapes=[
            pltpu.VMEM(shape, jnp.float32),
            pltpu.VMEM(tiles.shape, tiles.dtype),
            pltpu.VMEM(received.shape, received.dtype),
            pltpu.VMEM(shape, jnp.bfloat16),
            pltpu.SemaphoreType.DMA((2, GROUPS)),
            pltpu.SemaphoreType.DMA((ocean_count,)),
        ],
        compiler_params=pltpu.CompilerParams(vmem_limit_bytes=VMEM_LIMIT),
        cost_estimate=pl.CostEstimate(
            flops=4 * sources * columns * depth_k * shape[2],
            transcendentals=0,
            bytes_accessed=2 * sources * columns * depth_k,
        ),
        name="remap_packed",
    )(plan, *([total] if has_total else []), tiles, received)


def body(atm_fields, neighbours, send_slots, send_counts, tile_weights, tile_rows, tile_cols):
    block_count, column_count, cell_count = atm_fields.shape
    peers = lax.axis_size("gy")
    ocean_count = block_count // 4
    tile_count = tile_weights.shape[0]
    halo_width = block_count // 4
    slots = send_slots.reshape(peers, -1)
    own_counts = send_counts.reshape(peers)
    me = lax.axis_index("gy")

    def exchange(blocks):
        return lax.all_to_all(blocks, "gy", split_axis=0, concat_axis=0, tiled=True)

    doubled = own_counts >= 2
    before = jnp.cumsum(doubled.astype(jnp.int32))
    overflow = jnp.sum(jnp.where(doubled & (before == 1), slots[:, 1], 0))
    low, high = neighbour_blocks(atm_fields, halo_width)
    facts = jnp.stack([own_counts, before, jnp.broadcast_to(before[-1], before.shape)], axis=1)
    note = jnp.pad(facts.astype(atm_fields.dtype), ((0, 0), (0, cell_count - 3)))
    near = neighbours - (lax.axis_index(("gx", "gy")) * block_count - halo_width)
    where = jnp.concatenate([overflow[None] + halo_width, near[overflow]])
    near = near.reshape(-1)
    values = exchange(in_order(atm_fields, slots[:, 0], note))
    spares = lax.all_gather(
        one_payload(where, low, atm_fields, high), "gy", axis=0, tiled=True
    )
    slopes = gradients(slots[:, 0], near, low, atm_fields, high)
    slopes, values = lax.optimization_barrier((slopes, values))
    slopes = exchange(slopes)

    told = values[:, column_count, :3].astype(jnp.int32)
    arrived, rank = told[:, 0], told[:, 1]
    most = jnp.max(told[:, 2])
    planes = lax.axis_size("gx")
    ahead = [
        lax.ppermute(most, "gx", [(i, (i + step) % planes) for i in range(planes)])
        for step in range(1, planes)
    ]
    for other in ahead:
        most = jnp.maximum(most, other)
    slot_ids = lax.broadcasted_iota(jnp.int32, (2 * peers, tile_count), 0)
    codes = lax.broadcasted_iota(jnp.int32, (2 * peers, tile_count), 1) * 8 + tile_rows[None, :]
    named = slot_ids == tile_cols[None, :]
    first_code = jnp.min(jnp.where(named, codes, 8 * tile_count), axis=1).reshape(peers, 2)
    second_code = jnp.max(jnp.where(named, codes, -1), axis=1).reshape(peers, 2)

    def plan(live, slot):
        return jnp.concatenate([live.astype(jnp.int32), first_code[:, slot], second_code[:, slot]])

    plan_first = plan(arrived >= 1, 0)
    plan_spare = plan((arrived >= 2) & (rank == 1), 1)
    plan_rest = plan((arrived >= 2) & (rank > 1), 1)

    def add(this_plan, received, total, first_row, final=False):
        return remap(
            this_plan, received, tile_weights, total, first_row, ocean_count, column_count, final
        )

    total = add(plan_first, values, None, 0)
    total = add(plan_spare, spares, total, 0)

    tiles = pack(plan_first, tile_weights, cell_count, 2 * cell_count)
    done = remap_packed(plan_first, total, tiles, slopes, ocean_count, jnp.bfloat16)

    def with_rest(total, unused):
        rest_slopes = gradients(slots[:, 1], near, low, atm_fields, high)
        total = add(plan_rest, exchange(in_order(atm_fields, slots[:, 1], note)), total, 0)
        total = add(plan_rest, exchange(rest_slopes), total, cell_count)
        return add(plan_first, slopes, total, cell_count, final=True)

    return lax.cond(most > 1, with_rest, lambda unused, done: done, total, done)


def solution(mesh):
    return jax.shard_map(
        body,
        mesh=mesh,
        in_specs=(
            P(("gx", "gy"), None, None),
            P(("gx", "gy"), None),
            P(("gx", "gy"), None, None),
            P(("gx", "gy"), None),
            P(("gx", "gy"), None, None),
            P(("gx", "gy")),
            P(("gx", "gy")),
        ),
        out_specs=P(("gx", "gy"), None, None),
        check_vma=False,
    )
```
